32 devices in a mesh: groups: 2 (over x), isl: 16 (over z, y, core).
Axes of the slice: x: 2, y: 2, z: 4, core: 2. Of those that a mesh axis runs over, the one named last changes fastest.
Arguments:
- particles: bfloat16 [262144, 256], P(('groups', 'isl')), parts along dimension 0, may hold values from -6 to 6
- noise: bfloat16 [3, 262144, 256], P(None, ('groups', 'isl')), parts along dimension 1, may hold values from -3 to 3
- series: float32 [6, 256], P('groups'), parts along dimension 0, may hold values from -6 to 6
- transition: bfloat16 [256, 256], replicated, may hold values from -0.375 to 0.375
- obs_matrix: bfloat16 [256, 256], replicated, may hold values from -0.375 to 0.375
- precision: float32 [256], replicated, may hold values from 1 to 10
- src_island: int32 [3, 2048, 1], P(None, ('groups', 'isl')), parts along dimension 1, may hold values from 0 to 15; in each aligned block of 32 rows (0 to 31, 32 to 63, ..., all dimensions but the last counted through in order) at most 4 rows name the same one
- src_tile: int32 [3, 2048], P(None, ('groups', 'isl')), parts along dimension 1, may hold values from 0 to 63
- swap_bits: int32 [6], P('groups'), parts along dimension 0, may hold values from 0 to 3, as said below
Outputs:
- cloud: bfloat16 [262144, 256], P(('groups', 'isl')), parts along dimension 0
- first_moment: float32 [6, 256], P('groups'), parts along dimension 0
- second_moment: float32 [6, 256, 256], P('groups', 'isl'), parts along dimension 0
The draws below stay inside these ranges and needn't reach their ends.
There are 2 independent parts, one for each index of `groups`. The reference program is written for one: setup_inputs(seed, part) draws one part's arguments, and reference() takes and returns one part's arrays. A program takes and returns all parts, laid end to end along the dimension named above; an argument that names none is the same for every part. Nothing has to cross between parts.
Inputs may be any that keep to these rules, and one draw needn't show every extreme that they name: `src_island`: within each aligned block of 32 slots (half of one island's slots), no island is named more than 4 times; some island is named exactly that often. `swap_bits`: bits lie below log2(16); the top one occurs in every draw.
All inputs are finite; a program needn't handle non-finite values.
Results may differ from the reference program's by a relative error of at most 0.0085.
Values may be sent and summed in bfloat16 or wider, within the bound.
A program may use at most 128 MiB of HBM per device.

```python
import math
import jax
import jax.numpy as jnp
import numpy as np

D = 256
OBS = 256
TILE = 128
TILES_DEV = 64
STEPS = 3
CAP_HALF = 4
SLOTS = 1024
PART = 131072
N_ISL = 16


def draw_swap_bits(key, part):
    key = jax.random.fold_in(key, 7)
    top_bit = max(N_ISL.bit_length() - 1, 1)
    values = jax.random.randint(key, (STEPS,), 0, top_bit).astype(jnp.int32)
    return values.at[0].set(top_bit - 1)


def set_ends(entries, key, smallest, high):
    extent = entries.shape
    index_at = [jax.random.randint(jax.random.fold_in(key, axis), (), 0, extent[axis]) for axis in range(len(extent))]
    entries = entries.at[tuple(index_at)].set(smallest)
    longest = extent.index(max(extent))
    index_at[longest] = (index_at[longest] + 1) % extent[longest]
    return entries.at[tuple(index_at)].set(high)


def with_spikes(drawn, key, source, target, blocks, factor):
    def block_of(position):
        return (jnp.arange(drawn.shape[position]) // (drawn.shape[position] // blocks)).reshape((-1,) + (1,) * (drawn.ndim - 1 - position))

    first = jax.random.permutation(key, blocks)[block_of(target)]
    other_side = (block_of(target) + blocks // 2) % blocks
    return jnp.where((block_of(source) == first) | (block_of(source) == other_side), factor * drawn, drawn)


def shard_levels(own_key, shape, pieces, smallest, top_value):
    def one(dim, blocks):
        draws = jax.random.uniform(jax.random.fold_in(jax.random.fold_in(own_key, 6), dim), (blocks,), jnp.float32, smallest / len(pieces), top_value / len(pieces))
        return jnp.repeat(jnp.exp(draws), shape[dim] // blocks).reshape((-1,) + (1,) * (len(shape) - dim - 1))

    factor_of = one(*pieces[0])
    for cut in pieces[1:]:
        factor_of = factor_of * one(*cut)
    return factor_of


def routed_block(rng, own, number, rows, number_of, top, bound, lean):
    order = jax.random.permutation(rng, number_of)
    crowded, usual = shares(number_of, rows * top, bound, lean, True), shares(number_of, rows * top, bound, lean, False)
    places = jnp.arange(number_of)

    def named(tallies, offset_by):
        used = int((tallies > 0).sum())
        fixed = max(1, used // 4)
        shifted = fixed + (places - fixed + offset_by * (used - fixed)) % max(1, number_of - fixed)
        return jnp.zeros((number_of,), jnp.int32).at[order[jnp.where(places < fixed, places, shifted)]].set(jnp.asarray(tallies, jnp.int32))

    tallies = jnp.where(number % 4 == 0, named(crowded, number // 4), named(usual, number - number // 4 - 1))
    mixed = jax.random.permutation(jax.random.fold_in(own, 3), number_of)
    donor, taker = mixed[0:number_of // 2 * 2:2], mixed[1:number_of // 2 * 2:2]
    room = jnp.minimum(tallies[donor] - 1, bound - tallies[taker]) // 2
    room = jnp.where((donor == order[0]) | (taker == order[0]) | (tallies[taker] == 0), 0, jnp.maximum(room, 0))
    shifted = jax.random.randint(jax.random.fold_in(own, 4), (number_of // 2,), 0, 1 << 20) % (room + 1)
    tallies = tallies.at[donor].add(-shifted).at[taker].add(shifted)
    labels = jnp.searchsorted(jnp.cumsum(tallies), jnp.arange(rows * top), side="right").astype(jnp.int32)
    grid = labels.reshape(top, rows).T
    grid = grid[jax.random.permutation(jax.random.fold_in(own, 1), rows)]
    offset_by = jax.random.randint(jax.random.fold_in(own, 2), (rows, 1), 0, top)
    return jnp.take_along_axis(grid, (jnp.arange(top)[None, :] + offset_by) % top, axis=1)


def shares(amount, total, most, lean, full):
    portions = [(1 << 20) // math.isqrt(standing ** lean) + 1 for standing in range(1, amount + 1)]
    largest = most if full else min(most, max(-(-total // amount), total * portions[0] // sum(portions)))
    least = 1 if total - largest >= amount - 1 else 0
    holding, spare = [largest] + [least] * (amount - 1), total - largest - least * (amount - 1)
    while spare > 0:
        movable = [i for i in range(1, amount) if holding[i] < largest] or [i for i in range(1, amount) if holding[i] < most]
        mass, budget = sum([portions[i] for i in movable]), spare
        for i in movable:
            more = min(most - holding[i], max(1, budget * portions[i] // mass), spare)
            holding[i] = holding[i] + more
            spare = spare - more
    return np.array(holding)


def normal_values(key, extent, spread, bound, split=(), kind=jnp.bfloat16):
    entries = spread * jax.random.normal(key, extent, jnp.float32)
    if split:
        entries = entries * shard_levels(key, extent, split, -0.22, 0.18)
    return jnp.clip(entries, -bound, bound).astype(kind)


def noise_with(rng, shape, spread, most, pieces, heavy, kind=jnp.bfloat16):
    values = spread * jax.random.normal(rng, shape, jnp.float32)
    if pieces:
        values = values * shard_levels(rng, shape, pieces, -0.22, 0.18)
    return jnp.clip(with_spikes(values, jax.random.fold_in(rng, 3), *heavy), -most, most).astype(kind)


def setup_inputs(seed: int = 0, part: int = 0) -> dict:
    streams_of = jax.random.split(jax.random.key(seed), 10)
    part_splits = jax.random.split(jax.random.fold_in(streams_of[9], part), 10)
    particles = noise_with(part_splits[0], (PART, D), 1.0, 6.0, ((0, 16),), (0, 1, 16, 2.0))
    noise = normal_values(part_splits[1], (STEPS, PART, D), 0.5, 3.0, ((1, 16),))
    series = normal_values(part_splits[2], (STEPS, OBS), 1.0, 6.0, (), jnp.float32)
    transition = normal_values(streams_of[3], (D, D), D ** -0.5, 0.375)
    obs_matrix = normal_values(streams_of[4], (D, OBS), D ** -0.5, 0.375)
    precision = jnp.clip(jnp.exp(jax.random.uniform(streams_of[5], (OBS,), jnp.float32, math.log(1.0), math.log(10.0))), 1.0, 10.0)
    src_island_keys = jax.random.split(jax.random.fold_in(part_splits[6], 1), STEPS * SLOTS // (TILES_DEV // 2))
    src_island_turns = jax.random.permutation(jax.random.fold_in(part_splits[6], 3), STEPS * SLOTS // (TILES_DEV // 2))
    src_island = jax.vmap(lambda own, number: routed_block(jax.random.fold_in(part_splits[6], 2), own, number, TILES_DEV // 2, N_ISL, 1, CAP_HALF, 2))(src_island_keys, src_island_turns).reshape((STEPS, SLOTS, 1))
    src_tile = set_ends(jax.random.randint(part_splits[7], (STEPS, SLOTS), 0, TILES_DEV), jax.random.fold_in(part_splits[7], 1), 0, TILES_DEV - 1).astype(jnp.int32)
    swap_bits = draw_swap_bits(jax.random.fold_in(jax.random.fold_in(streams_of[9], part), 71), part)
    return {"particles": particles, "noise": noise, "series": series, "transition": transition, "obs_matrix": obs_matrix, "precision": precision, "src_island": src_island, "src_tile": src_tile, "swap_bits": swap_bits}


def reference(particles, noise, series, transition, obs_matrix, precision, src_island, src_tile, swap_bits):
    cloud = particles
    halfway = TILES_DEV // 2
    firsts = []
    seconds = []
    for step in range(STEPS):
        propagated = (jnp.dot(cloud, transition, preferred_element_type=jnp.float32) + noise[step].astype(jnp.float32)).astype(jnp.bfloat16)
        predicted = jnp.dot(propagated, obs_matrix, preferred_element_type=jnp.float32)
        innovation = series[step][None, :] - predicted
        likelihood = jnp.exp(-0.5 * jnp.mean(innovation * innovation * precision[None, :], axis=1))
        weight_total = jnp.sum(likelihood)
        first_sums = jnp.sum(propagated.astype(jnp.float32) * likelihood[:, None], axis=0)
        weighted = (propagated.astype(jnp.float32) * likelihood[:, None]).astype(jnp.bfloat16)
        second_sums = jnp.dot(weighted.T, propagated, preferred_element_type=jnp.float32)
        firsts.append(first_sums / weight_total)
        seconds.append(second_sums / weight_total)
        tiles = propagated.reshape(SLOTS, TILE, D)
        parent = (src_island[step, :, 0] * TILES_DEV + src_tile[step]).astype(jnp.int32)
        resampled = tiles[parent].reshape(N_ISL, TILES_DEV, TILE, D)
        bit_value = jnp.left_shift(jnp.int32(1), swap_bits[step].astype(jnp.int32))
        partner_order = jnp.bitwise_xor(jnp.arange(N_ISL, dtype=jnp.int32), bit_value)
        upper_tiles = resampled[partner_order, halfway:]
        cloud = jnp.concatenate([resampled[:, :halfway], upper_tiles], axis=1).reshape(PART, D)
    return cloud, jnp.stack(firsts), jnp.stack(seconds)
```

```python
import functools

import jax
import jax.numpy as jnp
from jax import lax
from jax.experimental import pallas as pl
from jax.experimental.pallas import tpu as pltpu
from jax.sharding import PartitionSpec as P

TILE = 128
STEPS = 3
CHUNK = 8
MESH = pl.DeviceIdType.MESH


def exchange_kernel(islands, per_peer, *refs):
    count = len(per_peer)
    sources, targets = refs[:count], refs[count : 2 * count]
    send_sems, recv_sems, own_sems = refs[2 * count :]
    me = lax.axis_index("isl")
    barrier = pltpu.get_barrier_semaphore()

    def greet(k, carry):
        pl.semaphore_signal(
            barrier, inc=1, device_id={"isl": lax.rem(me + k, islands)}, device_id_type=MESH
        )
        return carry

    lax.fori_loop(1, islands, greet, 0)
    pl.semaphore_wait(barrier, islands - 1)

    def remote(a, k):
        peer = lax.rem(me + k, islands)
        return pltpu.make_async_remote_copy(
            src_ref=sources[a].at[peer] if per_peer[a] else sources[a],
            dst_ref=targets[a].at[me],
            send_sem=send_sems.at[a, k],
            recv_sem=recv_sems.at[a, k],
            device_id={"isl": peer},
            device_id_type=MESH,
        )

    def own(a):
        return pltpu.make_async_copy(
            sources[a].at[me] if per_peer[a] else sources[a], targets[a].at[me], own_sems.at[a]
        )

    def send(k, carry):
        for a in range(count):
            remote(a, k).start()
        return carry

    lax.fori_loop(1, islands, send, 0)
    for a in range(count):
        own(a).start()

    def finish(k, carry):
        for a in range(count):
            remote(a, k).wait()
        return carry

    lax.fori_loop(1, islands, finish, 0)
    for a in range(count):
        own(a).wait()


def exchange(arrays, per_peer, islands, collective_id, name):
    shapes = [
        jax.ShapeDtypeStruct(x.shape if each else (islands,) + x.shape, x.dtype)
        for x, each in zip(arrays, per_peer)
    ]
    count = len(arrays)
    return pl.pallas_call(
        functools.partial(exchange_kernel, islands, per_peer),
        out_shape=shapes,
        in_specs=[pl.BlockSpec(memory_space=pl.ANY)] * count,
        out_specs=[pl.BlockSpec(memory_space=pl.ANY)] * count,
        scratch_shapes=[
            pltpu.SemaphoreType.DMA((count, islands)),
            pltpu.SemaphoreType.DMA((count, islands)),
            pltpu.SemaphoreType.DMA((count,)),
        ],
        compiler_params=pltpu.CompilerParams(collective_id=collective_id, has_side_effects=True),
        name=name,
    )(*arrays)


def filter_kernel(slots, source_ref, send_ref, *refs):
    tiles = refs[:CHUNK]
    noise_ref, series_ref, transition_ref, obs_ref, precision_ref = refs[CHUNK : CHUNK + 5]
    packed_ref, second_ref, stats_ref, moved, sem = refs[CHUNK + 5 :]
    i = pl.program_id(0)
    width = transition_ref.shape[0]

    @pl.when(i == 0)
    def _():
        second_ref[...] = jnp.zeros_like(second_ref)
        stats_ref[...] = jnp.zeros_like(stats_ref)

    cloud = jnp.concatenate([t[0] for t in tiles], axis=0)
    propagated = (
        jnp.dot(cloud, transition_ref[...], preferred_element_type=jnp.float32)
        + noise_ref[0].astype(jnp.float32)
    ).astype(jnp.bfloat16)
    moved[pl.ds(i * CHUNK, CHUNK)] = propagated.reshape(CHUNK, TILE, width)
    innovation = series_ref[...] - jnp.dot(
        propagated, obs_ref[...], preferred_element_type=jnp.float32
    )
    misfit = jnp.mean(innovation * innovation * precision_ref[...], axis=1, keepdims=True)
    likelihood = jnp.exp(-0.5 * misfit)
    scaled = propagated.astype(jnp.float32) * likelihood
    stats_ref[0:1, :] += jnp.sum(scaled, axis=0, keepdims=True)
    stats_ref[1:2, :] += jnp.broadcast_to(jnp.sum(likelihood, axis=0, keepdims=True), (1, width))
    second_ref[...] += lax.dot_general(
        scaled.astype(jnp.bfloat16),
        propagated,
        (((0,), (0,)), ((), ())),
        preferred_element_type=jnp.float32,
    )

    @pl.when(i == pl.num_programs(0) - 1)
    def _():
        def pack(k, carry):
            pltpu.make_async_copy(moved.at[send_ref[k]], packed_ref.at[k], sem).start()
            return carry

        lax.fori_loop(0, slots, pack, 0, unroll=8)
        pltpu.make_async_copy(packed_ref, packed_ref, sem).wait()


def filter_step(
    step, tiles, source, send, noise, series, transition, obs_matrix, precision, tile_count
):
    width = transition.shape[0]
    slots = send.shape[0]
    rows = CHUNK * TILE
    whole = lambda i, *_: (0, 0)
    tile_specs = [
        pl.BlockSpec((1, TILE, width), lambda i, source, send, t=t: (source[i * CHUNK + t], 0, 0))
        for t in range(CHUNK)
    ]
    matmuls = 3 * 2 * tile_count * TILE * width * width
    return pl.pallas_call(
        functools.partial(filter_kernel, slots),
        grid_spec=pltpu.PrefetchScalarGridSpec(
            num_scalar_prefetch=2,
            grid=(tile_count // CHUNK,),
            in_specs=tile_specs
            + [
                pl.BlockSpec((1, rows, width), lambda i, *_: (step, i, 0)),
                pl.BlockSpec((1, width), whole),
                pl.BlockSpec((width, width), whole),
                pl.BlockSpec((width, width), whole),
                pl.BlockSpec((1, width), whole),
            ],
            out_specs=[
                pl.BlockSpec(memory_space=pl.ANY),
                pl.BlockSpec((width, width), whole),
                pl.BlockSpec((8, width), whole),
            ],
            scratch_shapes=[
                pltpu.VMEM((tile_count, TILE, width), jnp.bfloat16),
                pltpu.SemaphoreType.DMA,
            ],
        ),
        out_shape=[
            jax.ShapeDtypeStruct((slots, TILE, width), jnp.bfloat16),
            jax.ShapeDtypeStruct((width, width), jnp.float32),
            jax.ShapeDtypeStruct((8, width), jnp.float32),
        ],
        compiler_params=pltpu.CompilerParams(vmem_limit_bytes=40 * 1024 * 1024),
        cost_estimate=pl.CostEstimate(
            flops=matmuls, bytes_accessed=5 * tile_count * TILE * width * 2, transcendentals=0
        ),
        name="filter_step",
    )(source, send, *([tiles] * CHUNK), noise, series, transition, obs_matrix, precision)


def place_kernel(source_ref, *refs):
    tiles, out_ref = refs[:CHUNK], refs[CHUNK]
    for t in range(CHUNK):
        out_ref[pl.ds(t * TILE, TILE), :] = tiles[t][0]


def place(tiles, source, tile_count):
    width = tiles.shape[2]
    return pl.pallas_call(
        place_kernel,
        grid_spec=pltpu.PrefetchScalarGridSpec(
            num_scalar_prefetch=1,
            grid=(tile_count // CHUNK,),
            in_specs=[
                pl.BlockSpec((1, TILE, width), lambda i, source, t=t: (source[i * CHUNK + t], 0, 0))
                for t in range(CHUNK)
            ],
            out_specs=pl.BlockSpec((CHUNK * TILE, width), lambda i, *_: (i, 0)),
        ),
        out_shape=jax.ShapeDtypeStruct((tile_count * TILE, width), tiles.dtype),
        compiler_params=pltpu.CompilerParams(vmem_limit_bytes=16 * 1024 * 1024),
        name="place_tiles",
    )(source, *([tiles] * CHUNK))


def plan(parents, swap_bits, own_index, capacity, islands, tile_count):
    halfway = tile_count // 2
    upper = parents[:, :, halfway:]
    swapped = upper
    for bit in range(max(islands.bit_length() - 1, 1)):
        span = 1 << bit
        if 2 * span > islands:
            break
        flipped = upper.reshape(STEPS, islands // (2 * span), 2, span, halfway)[:, :, ::-1]
        swapped = jnp.where(
            (swap_bits == bit)[:, None, None], flipped.reshape(upper.shape), swapped
        )
    wanted = jnp.concatenate([parents[:, :, :halfway], swapped], axis=2)
    island, tile = wanted // tile_count, wanted % tile_count
    before = jnp.arange(tile_count)[:, None] < jnp.arange(tile_count)[None, :]
    matches = island == own_index
    position = jnp.dot(
        matches.astype(jnp.bfloat16).reshape(STEPS * islands, tile_count),
        before.astype(jnp.bfloat16),
        preferred_element_type=jnp.float32,
    ).reshape(matches.shape)
    ranks = jnp.arange(capacity, dtype=jnp.float32)
    chosen = matches[:, :, None, :] & (position[:, :, None, :] == ranks[None, None, :, None])
    send = jnp.sum(jnp.where(chosen, tile[:, :, None, :], 0), axis=3)
    own = lax.dynamic_index_in_dim(island, own_index, 1, keepdims=False)
    same = (own[:, :, None] == own[:, None, :]) & before[None]
    source = own * capacity + jnp.sum(same.astype(jnp.int32), axis=1)
    return send.reshape(STEPS, islands * capacity), source


def local(
    particles, noise, series, transition, obs_matrix, precision, src_island, src_tile, swap_bits
):
    islands = lax.axis_size("isl")
    own_index = lax.axis_index("isl")
    row_count, width = particles.shape
    tile_count = row_count // TILE
    half_capacity = max(2, tile_count // islands)
    capacity = 2 * half_capacity
    table = src_island[:, :, 0] * tile_count + src_tile
    table = jnp.pad(table, ((0, 8 - STEPS), (0, 128 - tile_count)))
    (tables,) = exchange([table], [False], islands, 0, "share_tables")
    parents = jnp.swapaxes(tables[:, :STEPS, :tile_count], 0, 1)
    send, source = plan(parents, swap_bits, own_index, capacity, islands, tile_count)
    tiles = particles.reshape(tile_count, TILE, width)
    slot = jnp.arange(tile_count, dtype=jnp.int32)
    band = width // islands
    firsts, seconds = [], []
    for step in range(STEPS):
        packed, second, stats = filter_step(
            step,
            tiles,
            slot,
            send[step],
            noise,
            series[step : step + 1],
            transition,
            obs_matrix,
            precision[None, :],
            tile_count,
        )
        incoming, bands, all_stats = exchange(
            [
                packed.reshape(islands, capacity * TILE, width),
                second.reshape(islands, band, width),
                stats,
            ],
            [True, True, False],
            islands,
            1,
            "exchange_tiles",
        )
        tiles = incoming.reshape(islands * capacity, TILE, width)
        slot = source[step]
        total = jnp.sum(all_stats, axis=0)
        firsts.append(total[0] / total[1, 0])
        seconds.append(jnp.sum(bands, axis=0) / total[1, 0])
    cloud = place(tiles, slot, tile_count)
    return (cloud, jnp.stack(firsts), jnp.stack(seconds))


def solution(mesh):
    return jax.shard_map(
        local,
        mesh=mesh,
        in_specs=(
            P(("groups", "isl"), None),
            P(None, ("groups", "isl"), None),
            P("groups", None),
            P(),
            P(),
            P(),
            P(None, ("groups", "isl"), None),
            P(None, ("groups", "isl")),
            P("groups"),
        ),
        out_specs=(P(("groups", "isl"), None), P("groups", None), P("groups", "isl", None)),
        check_vma=False,
    )
```

```python
import functools

import jax
import jax.numpy as jnp
from jax import lax
from jax.experimental import pallas as pl
from jax.experimental.pallas import tpu as pltpu
from jax.sharding import PartitionSpec as P

TILE = 128
STEPS = 3
LANES = 128
CHUNK = 8
MESH = pl.DeviceIdType.MESH


def greet_all(total, me, where):
    barrier = pltpu.get_barrier_semaphore()

    def greet(k, carry):
        pl.semaphore_signal(
            barrier, inc=1, device_id=where(lax.rem(me + k, total)), device_id_type=MESH
        )
        return carry

    lax.fori_loop(1, total, greet, 0)
    pl.semaphore_wait(barrier, total - 1)


def share_kernel(total, islands, table_ref, all_ref, send_sems, recv_sems, own_sem):
    me = lax.axis_index("groups") * islands + lax.axis_index("isl")

    def where(peer):
        return (peer // islands, lax.rem(peer, islands))

    greet_all(total, me, where)

    def remote(k):
        return pltpu.make_async_remote_copy(
            src_ref=table_ref,
            dst_ref=all_ref.at[me],
            send_sem=send_sems.at[k],
            recv_sem=recv_sems.at[k],
            device_id=where(lax.rem(me + k, total)),
            device_id_type=MESH,
        )

    def send(k, carry):
        remote(k).start()
        return carry

    def finish(k, carry):
        remote(k).wait()
        return carry

    lax.fori_loop(1, total, send, 0)
    own = pltpu.make_async_copy(table_ref, all_ref.at[me], own_sem)
    own.start()
    lax.fori_loop(1, total, finish, 0)
    own.wait()


def share_tables(table, groups, islands):
    total = groups * islands
    return pl.pallas_call(
        functools.partial(share_kernel, total, islands),
        out_shape=jax.ShapeDtypeStruct((total,) + table.shape, table.dtype),
        in_specs=[pl.BlockSpec(memory_space=pl.ANY)],
        out_specs=pl.BlockSpec(memory_space=pl.ANY),
        scratch_shapes=[
            pltpu.SemaphoreType.DMA((total,)),
            pltpu.SemaphoreType.DMA((total,)),
            pltpu.SemaphoreType.DMA,
        ],
        compiler_params=pltpu.CompilerParams(collective_id=0, has_side_effects=True),
        name="share_tables",
    )(table)


def exchange_kernel(islands, kinds, *refs):
    count = len(kinds)
    sources, targets = refs[:count], refs[count : 2 * count]
    send_sems, recv_sems, own_sems = refs[2 * count :]
    me = lax.axis_index("isl")
    sibling = me + 1 - 2 * lax.rem(me, 2)
    greet_all(islands, me, lambda peer: {"isl": peer})

    def ends(a, k, peer):
        kind = kinds[a]
        if kind == "peer":
            return sources[a].at[peer], targets[a].at[me]
        if kind == "all":
            return sources[a], targets[a].at[me]
        rows = sources[a].shape[1]
        if kind == "half" and k % 2 == 1:
            rows -= TILE
        return sources[a].at[peer, pl.ds(0, rows)], targets[a].at[me, pl.ds(0, rows)]

    def remote(a, k):
        if kinds[a] == "pair":
            peer, (source, target) = sibling, (sources[a], targets[a].at[1])
        else:
            peer = lax.rem(me + k, islands)
            source, target = ends(a, k, peer)
        return pltpu.make_async_remote_copy(
            src_ref=source,
            dst_ref=target,
            send_sem=send_sems.at[a, k],
            recv_sem=recv_sems.at[a, k],
            device_id={"isl": peer},
            device_id_type=MESH,
        )

    def own(a):
        if kinds[a] == "pair":
            source, target = sources[a], targets[a].at[0]
        else:
            source, target = ends(a, 0, me)
        return pltpu.make_async_copy(source, target, own_sems.at[a])

    plans = [
        (a, k)
        for k in range(1, islands)
        for a in range(count)
        if (kinds[a] != "pair" or k == 1)
        and not (kinds[a] == "half" and k % 2 == 1 and sources[a].shape[1] == TILE)
    ]
    for a, k in plans:
        remote(a, k).start()
    for a in range(count):
        own(a).start()
    for a, k in plans:
        remote(a, k).wait()
    for a in range(count):
        own(a).wait()


def exchange(arrays, kinds, shapes, islands, collective_id, name):
    count = len(arrays)
    return pl.pallas_call(
        functools.partial(exchange_kernel, islands, kinds),
        out_shape=[jax.ShapeDtypeStruct(dims, x.dtype) for x, dims in zip(arrays, shapes)],
        in_specs=[pl.BlockSpec(memory_space=pl.ANY)] * count,
        out_specs=[pl.BlockSpec(memory_space=pl.ANY)] * count,
        scratch_shapes=[
            pltpu.SemaphoreType.DMA((count, islands)),
            pltpu.SemaphoreType.DMA((count, islands)),
            pltpu.SemaphoreType.DMA((count,)),
        ],
        compiler_params=pltpu.CompilerParams(collective_id=collective_id, has_side_effects=True),
        name=name,
    )(*arrays)


def fetch(first_ref, second_ref, index, target, sem):
    split = first_ref.shape[0]

    @pl.when(index < split)
    def _():
        pltpu.make_async_copy(first_ref.at[index], target, sem).start()

    @pl.when(index >= split)
    def _():
        pltpu.make_async_copy(second_ref.at[index - split], target, sem).start()


def filter_kernel(source_ref, send_ref, spare_ref, first_ref, other_ref, *refs):
    noise_ref, series_ref, transition_ref, obs_ref, precision_ref = refs[:5]
    packed_ref, excess_ref, second_ref, stats_ref, fetched, moved, fetch_sems, sem = refs[5:]
    i = pl.program_id(0)

    def prefetch(chunk, slot):
        for t in range(CHUNK):
            index = source_ref[chunk * CHUNK + t]
            fetch(first_ref, other_ref, index, fetched.at[slot, t], fetch_sems.at[slot])

    now = lax.rem(i, 2)

    @pl.when(i == 0)
    def _():
        prefetch(0, 0)

    @pl.when(i + 1 < pl.num_programs(0))
    def _():
        prefetch(i + 1, 1 - now)

    pltpu.make_async_copy(fetched.at[now], fetched.at[now], fetch_sems.at[now]).wait()
    width = transition_ref.shape[0]

    @pl.when(i == 0)
    def _():
        second_ref[...] = jnp.zeros_like(second_ref)
        stats_ref[...] = jnp.zeros_like(stats_ref)

    cloud = fetched[now].reshape(CHUNK * TILE, width)
    propagated = (
        jnp.dot(cloud, transition_ref[...], preferred_element_type=jnp.float32)
        + noise_ref[0].astype(jnp.float32)
    ).astype(jnp.bfloat16)
    moved[pl.ds(i * CHUNK, CHUNK)] = propagated.reshape(CHUNK, TILE, width)
    innovation = series_ref[...] - jnp.dot(
        propagated, obs_ref[...], preferred_element_type=jnp.float32
    )
    misfit = jnp.mean(innovation * innovation * precision_ref[...], axis=1, keepdims=True)
    likelihood = jnp.exp(-0.5 * misfit)
    scaled = propagated.astype(jnp.float32) * likelihood
    sums = jnp.sum(scaled, axis=0, keepdims=True)
    pieces = width // LANES
    for c in range(pieces):
        stats_ref[c : c + 1, :] += sums[:, c * LANES : (c + 1) * LANES]
    stats_ref[pieces : pieces + 1, :] += jnp.broadcast_to(
        jnp.sum(likelihood, axis=0, keepdims=True), (1, LANES)
    )
    second_ref[...] += lax.dot_general(
        scaled.astype(jnp.bfloat16),
        propagated,
        (((0,), (0,)), ((), ())),
        preferred_element_type=jnp.float32,
    )

    @pl.when(i == pl.num_programs(0) - 1)
    def _():
        def pack(k, carry):
            pltpu.make_async_copy(moved.at[send_ref[k]], packed_ref.at[k], sem.at[0]).start()
            return carry

        def pack_excess(k, carry):
            pltpu.make_async_copy(moved.at[spare_ref[k]], excess_ref.at[k], sem.at[1]).start()
            return carry

        lax.fori_loop(0, packed_ref.shape[0], pack, 0, unroll=8)
        lax.fori_loop(0, excess_ref.shape[0], pack_excess, 0, unroll=8)
        pltpu.make_async_copy(packed_ref, packed_ref, sem.at[0]).wait()
        pltpu.make_async_copy(excess_ref, excess_ref, sem.at[1]).wait()


def filter_step(
    step, first, other, source, send, spare, noise, series, transition, obs_matrix, precision
):
    width = transition.shape[0]
    tile_count = source.shape[0]
    rows = CHUNK * TILE
    whole = lambda i, *_: (0, 0)
    matmuls = 3 * 2 * tile_count * TILE * width * width
    return pl.pallas_call(
        filter_kernel,
        grid_spec=pltpu.PrefetchScalarGridSpec(
            num_scalar_prefetch=3,
            grid=(tile_count // CHUNK,),
            in_specs=[
                pl.BlockSpec(memory_space=pl.ANY),
                pl.BlockSpec(memory_space=pl.ANY),
                pl.BlockSpec((1, rows, width), lambda i, *_: (step, i, 0)),
                pl.BlockSpec((1, width), whole),
                pl.BlockSpec((width, width), whole),
                pl.BlockSpec((width, width), whole),
                pl.BlockSpec((1, width), whole),
            ],
            out_specs=[
                pl.BlockSpec(memory_space=pl.ANY),
                pl.BlockSpec(memory_space=pl.ANY),
                pl.BlockSpec((width, width), whole),
                pl.BlockSpec((8, LANES), whole),
            ],
            scratch_shapes=[
                pltpu.VMEM((2, CHUNK, TILE, width), jnp.bfloat16),
                pltpu.VMEM((tile_count, TILE, width), jnp.bfloat16),
                pltpu.SemaphoreType.DMA((2,)),
                pltpu.SemaphoreType.DMA((2,)),
            ],
        ),
        out_shape=[
            jax.ShapeDtypeStruct((send.shape[0], TILE, width), jnp.bfloat16),
            jax.ShapeDtypeStruct((spare.shape[0], TILE, width), jnp.bfloat16),
            jax.ShapeDtypeStruct((width, width), jnp.float32),
            jax.ShapeDtypeStruct((8, LANES), jnp.float32),
        ],
        compiler_params=pltpu.CompilerParams(vmem_limit_bytes=40 * 1024 * 1024),
        cost_estimate=pl.CostEstimate(
            flops=matmuls, bytes_accessed=5 * tile_count * TILE * width * 2, transcendentals=0
        ),
        name="filter_step",
    )(source, send, spare, first, other, noise, series, transition, obs_matrix, precision)


def place_kernel(source_ref, first_ref, other_ref, out_ref, sem):
    def move(k, carry):
        fetch(first_ref, other_ref, source_ref[k], out_ref.at[k], sem)
        return carry

    lax.fori_loop(0, out_ref.shape[0], move, 0)
    pltpu.make_async_copy(out_ref, out_ref, sem).wait()


def place(first, other, source, name):
    return pl.pallas_call(
        place_kernel,
        grid_spec=pltpu.PrefetchScalarGridSpec(
            num_scalar_prefetch=1,
            grid=(1,),
            in_specs=[pl.BlockSpec(memory_space=pl.ANY)] * 2,
            out_specs=pl.BlockSpec(memory_space=pl.ANY),
            scratch_shapes=[pltpu.SemaphoreType.DMA],
        ),
        out_shape=jax.ShapeDtypeStruct(source.shape + first.shape[1:], first.dtype),
        name=name,
    )(source, first, other)


def swap_upper(parents, bits, islands, halfway):
    upper = parents[:, :, halfway:]
    swapped = upper
    for bit in range(max(islands.bit_length() - 1, 1)):
        span = 1 << bit
        flipped = upper.reshape(-1, islands // (2 * span), 2, span, halfway)[:, :, ::-1]
        swapped = jnp.where((bits == bit)[:, None, None], flipped.reshape(upper.shape), swapped)
    return jnp.concatenate([parents[:, :, :halfway], swapped], axis=2)


def plan(tables, bits, group, me, islands, tile_count, direct, capacity):
    groups = bits.shape[0]
    spare = capacity - direct
    wanted = swap_upper(
        tables.reshape(groups * STEPS, islands, tile_count),
        bits.reshape(groups * STEPS),
        islands,
        tile_count // 2,
    )
    island_of = wanted // tile_count
    ids = jnp.arange(islands, dtype=jnp.int32)
    counts = jnp.sum((island_of[:, :, None, :] == ids[:, None]).astype(jnp.int32), axis=3)
    over = jnp.maximum(counts - direct, 0)
    by_chip = jnp.sum(over.reshape(groups, STEPS, islands, islands // 2, 2), axis=4)
    need = jnp.max(by_chip, axis=(0, 2, 3))

    mine = lambda x: lax.dynamic_index_in_dim(
        x.reshape((groups, STEPS) + x.shape[1:]), group, 0, keepdims=False
    )
    island, tile, over = mine(island_of), mine(wanted % tile_count), mine(over)
    before = jnp.arange(tile_count)[:, None] < jnp.arange(tile_count)[None, :]
    matches = island == me
    position = jnp.dot(
        matches.astype(jnp.bfloat16).reshape(STEPS * islands, tile_count),
        before.astype(jnp.bfloat16),
        preferred_element_type=jnp.float32,
    ).reshape(matches.shape)
    ranks = jnp.arange(capacity, dtype=jnp.float32)
    chosen = matches[:, :, None, :] & (position[:, :, None, :] == ranks[None, None, :, None])
    send = jnp.sum(jnp.where(chosen, tile[:, :, None, :], 0), axis=3)

    core = me % 2
    of_even = lax.dynamic_index_in_dim(over, me - core, 2, keepdims=False)[:, :, None]
    order = 2 * jnp.arange(spare, dtype=jnp.int32)[None, :] + ((core + ids) % 2)[:, None]
    from_odd = (order[None] >= of_even).astype(jnp.int32)
    rank = jnp.clip(order[None] - from_odd * of_even, 0, spare - 1)
    carried = (from_odd != core).astype(jnp.int32) * (islands * spare) + ids[:, None] * spare + rank

    own = lax.dynamic_index_in_dim(island, me, 1, keepdims=False)
    same = (own[:, :, None] == own[:, None, :]) & before[None]
    own_rank = jnp.sum(same.astype(jnp.int32), axis=1)
    to_me = lax.dynamic_index_in_dim(over, me, 1, keepdims=False)
    even_over = jnp.pad(to_me[:, :-1], ((0, 0), (1, 0))) * (ids % 2)
    offset = jnp.sum(jnp.where(own[:, :, None] == ids, even_over[:, None, :], 0), axis=2)
    later = own_rank - direct + offset
    carrier = own - own % 2 + (later + me) % 2
    source = jnp.where(
        own_rank < direct,
        own * direct + own_rank,
        islands * direct + carrier * spare + later // 2,
    )
    return (
        need,
        send[:, :, :direct].reshape(STEPS, -1),
        send[:, :, direct:].reshape(STEPS, -1),
        carried,
        source,
    )


def local(
    particles, noise, series, transition, obs_matrix, precision, src_island, src_tile, swap_bits
):
    groups, islands = lax.axis_size("groups"), lax.axis_size("isl")
    group, me = lax.axis_index("groups"), lax.axis_index("isl")
    row_count, width = particles.shape
    tile_count = row_count // TILE
    capacity = 2 * max(2, tile_count // islands)
    direct = capacity // 2
    spare = capacity - direct
    table = src_island[:, :, 0] * tile_count + src_tile
    table = jnp.concatenate([table, swap_bits[:, None]], axis=1)
    table = jnp.pad(table, ((0, 8 - STEPS), (0, LANES - 1 - tile_count)))
    tables = share_tables(table, groups, islands).reshape(groups, islands, 8, LANES)
    bits = tables[:, 0, :STEPS, tile_count]
    parents = jnp.swapaxes(tables[:, :, :STEPS, :tile_count], 1, 2)
    need, send, excess_of, carried, source = plan(
        parents, bits, group, me, islands, tile_count, direct, capacity
    )
    first = other = particles.reshape(tile_count, TILE, width)
    slot = jnp.arange(tile_count, dtype=jnp.int32)
    band = width // islands
    pieces = width // LANES
    moment_type = jnp.bfloat16 if band % 16 == 0 else jnp.float32
    levels = [spare, spare + 1, spare + 2, 2 * spare]
    levels = sorted(set(min(x, 2 * spare) for x in levels))

    def second_exchange(number, pair, chosen):
        level = levels[number]
        most = (level + 1) // 2
        packed = place(pair, pair, chosen[:, :most].reshape(-1), "pack_spare")
        return exchange(
            [packed.reshape(islands, most * TILE, width)],
            ["half" if level % 2 else "peer_rows"],
            [(islands, spare * TILE, width)],
            islands,
            2 + number,
            "exchange_spare",
        )[0]

    firsts, seconds = [], []
    for step in range(STEPS):
        packed, excess, second, stats = filter_step(
            step,
            first,
            other,
            slot,
            send[step],
            excess_of[step],
            noise,
            series[step : step + 1],
            transition,
            obs_matrix,
            precision[None, :],
        )
        incoming, pair, bands, all_stats = exchange(
            [
                packed.reshape(islands, direct * TILE, width),
                excess,
                second.reshape(islands, band, width).astype(moment_type),
                stats,
            ],
            ["peer", "pair", "peer", "all"],
            [
                (islands, direct * TILE, width),
                (2,) + excess.shape,
                (islands, band, width),
                (islands,) + stats.shape,
            ],
            islands,
            1,
            "exchange_tiles",
        )
        level = sum((need[step] > x).astype(jnp.int32) for x in levels[:-1])
        later = lax.switch(
            level,
            [functools.partial(second_exchange, number) for number in range(len(levels))],
            pair.reshape((-1,) + excess.shape[1:]),
            carried[step],
        )
        first = incoming.reshape(islands * direct, TILE, width)
        other = later.reshape(islands * spare, TILE, width)
        slot = source[step]
        total = jnp.sum(all_stats, axis=0)
        firsts.append(total[:pieces].reshape(width) / total[pieces, 0])
        seconds.append(jnp.sum(bands.astype(jnp.float32), axis=0) / total[pieces, 0])
    cloud = place(first, other, slot, "place_tiles").reshape(row_count, width)
    return (cloud, jnp.stack(firsts), jnp.stack(seconds))


def solution(mesh):
    return jax.shard_map(
        local,
        mesh=mesh,
        in_specs=(
            P(("groups", "isl"), None),
            P(None, ("groups", "isl"), None),
            P("groups", None),
            P(),
            P(),
            P(),
            P(None, ("groups", "isl"), None),
            P(None, ("groups", "isl")),
            P("groups"),
        ),
        out_specs=(P(("groups", "isl"), None), P("groups", None), P("groups", "isl", None)),
        check_vma=False,
    )
```

```python
import functools

import jax
import jax.numpy as jnp
from jax import lax
from jax.experimental import pallas as pl
from jax.experimental.pallas import tpu as pltpu
from jax.sharding import PartitionSpec as P

TILE = 128
STEPS = 3
LANES = 128
CHUNK = 8
MESH = pl.DeviceIdType.MESH


def greet_all(total, me, where):
    barrier = pltpu.get_barrier_semaphore()

    def greet(k, carry):
        pl.semaphore_signal(
            barrier, inc=1, device_id=where(lax.rem(me + k, total)), device_id_type=MESH
        )
        return carry

    lax.fori_loop(1, total, greet, 0)
    pl.semaphore_wait(barrier, total - 1)


def share_kernel(total, islands, table_ref, all_ref, send_sems, recv_sems, own_sem):
    me = lax.axis_index("groups") * islands + lax.axis_index("isl")

    def where(peer):
        return (peer // islands, lax.rem(peer, islands))

    greet_all(total, me, where)

    def remote(k):
        return pltpu.make_async_remote_copy(
            src_ref=table_ref,
            dst_ref=all_ref.at[me],
            send_sem=send_sems.at[k],
            recv_sem=recv_sems.at[k],
            device_id=where(lax.rem(me + k, total)),
            device_id_type=MESH,
        )

    def send(k, carry):
        remote(k).start()
        return carry

    def finish(k, carry):
        remote(k).wait()
        return carry

    lax.fori_loop(1, total, send, 0)
    own = pltpu.make_async_copy(table_ref, all_ref.at[me], own_sem)
    own.start()
    lax.fori_loop(1, total, finish, 0)
    own.wait()


def share_tables(table, groups, islands):
    total = groups * islands
    return pl.pallas_call(
        functools.partial(share_kernel, total, islands),
        out_shape=jax.ShapeDtypeStruct((total,) + table.shape, table.dtype),
        in_specs=[pl.BlockSpec(memory_space=pl.ANY)],
        out_specs=pl.BlockSpec(memory_space=pl.ANY),
        scratch_shapes=[
            pltpu.SemaphoreType.DMA((total,)),
            pltpu.SemaphoreType.DMA((total,)),
            pltpu.SemaphoreType.DMA,
        ],
        compiler_params=pltpu.CompilerParams(collective_id=0, has_side_effects=True),
        name="share_tables",
    )(table)


def exchange_kernel(islands, kinds, *refs):
    count = len(kinds)
    sources, targets = refs[:count], refs[count : 2 * count]
    send_sems, recv_sems, own_sems = refs[2 * count :]
    me = lax.axis_index("isl")
    sibling = me + 1 - 2 * lax.rem(me, 2)
    greet_all(islands, me, lambda peer: {"isl": peer})

    def ends(a, k, peer):
        kind = kinds[a]
        if kind == "peer":
            return sources[a].at[peer], targets[a].at[me]
        if kind == "all":
            return sources[a], targets[a].at[me]
        rows = sources[a].shape[1]
        if kind == "half" and k % 2 == 1:
            rows -= TILE
        return sources[a].at[peer, pl.ds(0, rows)], targets[a].at[me, pl.ds(0, rows)]

    def remote(a, k):
        if kinds[a] == "pair":
            peer, source, target = sibling, sources[a], targets[a]
        else:
            peer = lax.rem(me + k, islands)
            source, target = ends(a, k, peer)
        return pltpu.make_async_remote_copy(
            src_ref=source,
            dst_ref=target,
            send_sem=send_sems.at[a, k],
            recv_sem=recv_sems.at[a, k],
            device_id={"isl": peer},
            device_id_type=MESH,
        )

    def own(a):
        source, target = ends(a, 0, me)
        return pltpu.make_async_copy(source, target, own_sems.at[a])

    plans = [
        (a, k)
        for k in range(1, islands)
        for a in range(count)
        if (kinds[a] != "pair" or k == 1)
        and not (kinds[a] == "half" and k % 2 == 1 and sources[a].shape[1] == TILE)
    ]
    for a, k in plans:
        remote(a, k).start()
    kept = [a for a in range(count) if kinds[a] != "pair"]
    for a in kept:
        own(a).start()
    for a, k in plans:
        remote(a, k).wait()
    for a in kept:
        own(a).wait()


def exchange(arrays, kinds, shapes, islands, collective_id, name):
    count = len(arrays)
    return pl.pallas_call(
        functools.partial(exchange_kernel, islands, kinds),
        out_shape=[jax.ShapeDtypeStruct(dims, x.dtype) for x, dims in zip(arrays, shapes)],
        in_specs=[pl.BlockSpec(memory_space=pl.ANY)] * count,
        out_specs=[pl.BlockSpec(memory_space=pl.ANY)] * count,
        scratch_shapes=[
            pltpu.SemaphoreType.DMA((count, islands)),
            pltpu.SemaphoreType.DMA((count, islands)),
            pltpu.SemaphoreType.DMA((count,)),
        ],
        compiler_params=pltpu.CompilerParams(collective_id=collective_id, has_side_effects=True),
        name=name,
    )(*arrays)


def fetch(first_ref, second_ref, index, target, sem):
    split = first_ref.shape[0]

    @pl.when(index < split)
    def _():
        pltpu.make_async_copy(first_ref.at[index], target, sem).start()

    @pl.when(index >= split)
    def _():
        pltpu.make_async_copy(second_ref.at[index - split], target, sem).start()


def filter_kernel(source_ref, send_ref, spare_ref, first_ref, other_ref, *refs):
    noise_ref, series_ref, transition_ref, obs_ref, precision_ref = refs[:5]
    packed_ref, excess_ref, second_ref, stats_ref, fetched, moved, fetch_sems, sem = refs[5:]
    i = pl.program_id(0)

    def prefetch(chunk, slot):
        for t in range(CHUNK):
            index = source_ref[chunk * CHUNK + t]
            fetch(first_ref, other_ref, index, fetched.at[slot, t], fetch_sems.at[slot])

    now = lax.rem(i, 2)

    @pl.when(i == 0)
    def _():
        prefetch(0, 0)

    @pl.when(i + 1 < pl.num_programs(0))
    def _():
        prefetch(i + 1, 1 - now)

    pltpu.make_async_copy(fetched.at[now], fetched.at[now], fetch_sems.at[now]).wait()
    width = transition_ref.shape[0]

    @pl.when(i == 0)
    def _():
        second_ref[...] = jnp.zeros_like(second_ref)
        stats_ref[...] = jnp.zeros_like(stats_ref)

    cloud = fetched[now].reshape(CHUNK * TILE, width)
    propagated = (
        jnp.dot(cloud, transition_ref[...], preferred_element_type=jnp.float32)
        + noise_ref[0].astype(jnp.float32)
    ).astype(jnp.bfloat16)
    moved[pl.ds(i * CHUNK, CHUNK)] = propagated.reshape(CHUNK, TILE, width)
    innovation = series_ref[...] - jnp.dot(
        propagated, obs_ref[...], preferred_element_type=jnp.float32
    )
    misfit = jnp.mean(innovation * innovation * precision_ref[...], axis=1, keepdims=True)
    likelihood = jnp.exp(-0.5 * misfit)
    scaled = propagated.astype(jnp.float32) * likelihood
    sums = jnp.sum(scaled, axis=0, keepdims=True)
    pieces = width // LANES
    for c in range(pieces):
        stats_ref[c : c + 1, :] += sums[:, c * LANES : (c + 1) * LANES]
    stats_ref[pieces : pieces + 1, :] += jnp.broadcast_to(
        jnp.sum(likelihood, axis=0, keepdims=True), (1, LANES)
    )
    second_ref[...] += lax.dot_general(
        scaled.astype(jnp.bfloat16),
        propagated,
        (((0,), (0,)), ((), ())),
        preferred_element_type=jnp.float32,
    )

    @pl.when(i == pl.num_programs(0) - 1)
    def _():
        def pack(k, carry):
            pltpu.make_async_copy(moved.at[send_ref[k]], packed_ref.at[k], sem.at[0]).start()
            return carry

        def pack_excess(k, carry):
            pltpu.make_async_copy(moved.at[spare_ref[k]], excess_ref.at[k], sem.at[1]).start()
            return carry

        lax.fori_loop(0, packed_ref.shape[0], pack, 0, unroll=8)
        lax.fori_loop(0, excess_ref.shape[0], pack_excess, 0, unroll=8)
        pltpu.make_async_copy(packed_ref, packed_ref, sem.at[0]).wait()
        pltpu.make_async_copy(excess_ref, excess_ref, sem.at[1]).wait()


def filter_step(
    step, first, other, source, send, spare, noise, series, transition, obs_matrix, precision
):
    width = transition.shape[0]
    tile_count = source.shape[0]
    rows = CHUNK * TILE
    whole = lambda i, *_: (0, 0)
    matmuls = 3 * 2 * tile_count * TILE * width * width
    return pl.pallas_call(
        filter_kernel,
        grid_spec=pltpu.PrefetchScalarGridSpec(
            num_scalar_prefetch=3,
            grid=(tile_count // CHUNK,),
            in_specs=[
                pl.BlockSpec(memory_space=pl.ANY),
                pl.BlockSpec(memory_space=pl.ANY),
                pl.BlockSpec((1, rows, width), lambda i, *_: (step, i, 0)),
                pl.BlockSpec((1, width), whole),
                pl.BlockSpec((width, width), whole),
                pl.BlockSpec((width, width), whole),
                pl.BlockSpec((1, width), whole),
            ],
            out_specs=[
                pl.BlockSpec(memory_space=pl.ANY),
                pl.BlockSpec(memory_space=pl.ANY),
                pl.BlockSpec((width, width), whole),
                pl.BlockSpec((8, LANES), whole),
            ],
            scratch_shapes=[
                pltpu.VMEM((2, CHUNK, TILE, width), jnp.bfloat16),
                pltpu.VMEM((tile_count, TILE, width), jnp.bfloat16),
                pltpu.SemaphoreType.DMA((2,)),
                pltpu.SemaphoreType.DMA((2,)),
            ],
        ),
        out_shape=[
            jax.ShapeDtypeStruct((send.shape[0], TILE, width), jnp.bfloat16),
            jax.ShapeDtypeStruct((spare.shape[0], TILE, width), jnp.bfloat16),
            jax.ShapeDtypeStruct((width, width), jnp.float32),
            jax.ShapeDtypeStruct((8, LANES), jnp.float32),
        ],
        compiler_params=pltpu.CompilerParams(vmem_limit_bytes=40 * 1024 * 1024),
        cost_estimate=pl.CostEstimate(
            flops=matmuls, bytes_accessed=5 * tile_count * TILE * width * 2, transcendentals=0
        ),
        name="filter_step",
    )(source, send, spare, first, other, noise, series, transition, obs_matrix, precision)


def place_kernel(source_ref, first_ref, other_ref, out_ref, fetched, sems):
    i = pl.program_id(0)

    def prefetch(chunk, slot):
        for t in range(CHUNK):
            index = source_ref[chunk * CHUNK + t]
            fetch(first_ref, other_ref, index, fetched.at[slot, t], sems.at[slot])

    now = lax.rem(i, 2)

    @pl.when(i == 0)
    def _():
        prefetch(0, 0)

    @pl.when(i + 1 < pl.num_programs(0))
    def _():
        prefetch(i + 1, 1 - now)

    pltpu.make_async_copy(fetched.at[now], fetched.at[now], sems.at[now]).wait()
    out_ref[...] = fetched[now]


def place(first, other, source, name):
    tile = first.shape[1:]
    return pl.pallas_call(
        place_kernel,
        grid_spec=pltpu.PrefetchScalarGridSpec(
            num_scalar_prefetch=1,
            grid=(source.shape[0] // CHUNK,),
            in_specs=[pl.BlockSpec(memory_space=pl.ANY)] * 2,
            out_specs=pl.BlockSpec((CHUNK,) + tile, lambda i, *_: (i, 0, 0)),
            scratch_shapes=[
                pltpu.VMEM((2, CHUNK) + tile, first.dtype),
                pltpu.SemaphoreType.DMA((2,)),
            ],
        ),
        out_shape=jax.ShapeDtypeStruct(source.shape + tile, first.dtype),
        compiler_params=pltpu.CompilerParams(vmem_limit_bytes=16 * 1024 * 1024),
        name=name,
    )(source, first, other)


def swap_upper(parents, bits, islands, halfway):
    upper = parents[:, :, halfway:]
    swapped = upper
    for bit in range(max(islands.bit_length() - 1, 1)):
        span = 1 << bit
        flipped = upper.reshape(-1, islands // (2 * span), 2, span, halfway)[:, :, ::-1]
        swapped = jnp.where((bits == bit)[:, None, None], flipped.reshape(upper.shape), swapped)
    return jnp.concatenate([parents[:, :, :halfway], swapped], axis=2)


def plan(tables, bits, group, me, islands, tile_count, direct, capacity):
    groups = bits.shape[0]
    spare = capacity - direct
    wanted = swap_upper(
        tables.reshape(groups * STEPS, islands, tile_count),
        bits.reshape(groups * STEPS),
        islands,
        tile_count // 2,
    )
    island_of = wanted // tile_count
    ids = jnp.arange(islands, dtype=jnp.int32)
    counts = jnp.sum((island_of[:, :, None, :] == ids[:, None]).astype(jnp.int32), axis=3)
    over = jnp.maximum(counts - direct, 0)
    by_chip = jnp.sum(over.reshape(groups, STEPS, islands, islands // 2, 2), axis=4)
    need = jnp.max(by_chip, axis=(0, 2, 3))

    mine = lambda x: lax.dynamic_index_in_dim(
        x.reshape((groups, STEPS) + x.shape[1:]), group, 0, keepdims=False
    )
    island, tile, over = mine(island_of), mine(wanted % tile_count), mine(over)
    before = jnp.arange(tile_count)[:, None] < jnp.arange(tile_count)[None, :]
    matches = island == me
    position = jnp.dot(
        matches.astype(jnp.bfloat16).reshape(STEPS * islands, tile_count),
        before.astype(jnp.bfloat16),
        preferred_element_type=jnp.float32,
    ).reshape(matches.shape)
    ranks = jnp.arange(capacity, dtype=jnp.float32)
    chosen = matches[:, :, None, :] & (position[:, :, None, :] == ranks[None, None, :, None])
    send = jnp.sum(jnp.where(chosen, tile[:, :, None, :], 0), axis=3)

    core = me % 2
    of_even = lax.dynamic_index_in_dim(over, me - core, 2, keepdims=False)[:, :, None]
    order = 2 * jnp.arange(spare, dtype=jnp.int32)[None, :] + ((core + ids) % 2)[:, None]
    from_odd = (order[None] >= of_even).astype(jnp.int32)
    rank = jnp.clip(order[None] - from_odd * of_even, 0, spare - 1)
    carried = (from_odd != core).astype(jnp.int32) * (islands * spare) + ids[:, None] * spare + rank

    own = lax.dynamic_index_in_dim(island, me, 1, keepdims=False)
    same = (own[:, :, None] == own[:, None, :]) & before[None]
    own_rank = jnp.sum(same.astype(jnp.int32), axis=1)
    to_me = lax.dynamic_index_in_dim(over, me, 1, keepdims=False)
    even_over = jnp.pad(to_me[:, :-1], ((0, 0), (1, 0))) * (ids % 2)
    offset = jnp.sum(jnp.where(own[:, :, None] == ids, even_over[:, None, :], 0), axis=2)
    later = own_rank - direct + offset
    carrier = own - own % 2 + (later + me) % 2
    source = jnp.where(
        own_rank < direct,
        own * direct + own_rank,
        islands * direct + carrier * spare + later // 2,
    )
    return (
        need,
        send[:, :, :direct].reshape(STEPS, -1),
        send[:, :, direct:].reshape(STEPS, -1),
        carried,
        source,
    )


def local(
    particles, noise, series, transition, obs_matrix, precision, src_island, src_tile, swap_bits
):
    groups, islands = lax.axis_size("groups"), lax.axis_size("isl")
    group, me = lax.axis_index("groups"), lax.axis_index("isl")
    row_count, width = particles.shape
    tile_count = row_count // TILE
    capacity = 2 * max(2, tile_count // islands)
    direct = capacity // 2
    spare = capacity - direct
    table = src_island[:, :, 0] * tile_count + src_tile
    table = jnp.concatenate([table, swap_bits[:, None]], axis=1)
    table = jnp.pad(table, ((0, 8 - STEPS), (0, LANES - 1 - tile_count)))
    tables = share_tables(table, groups, islands).reshape(groups, islands, 8, LANES)
    bits = tables[:, 0, :STEPS, tile_count]
    parents = jnp.swapaxes(tables[:, :, :STEPS, :tile_count], 1, 2)
    need, send, excess_of, carried, source = plan(
        parents, bits, group, me, islands, tile_count, direct, capacity
    )
    first = other = particles.reshape(tile_count, TILE, width)
    slot = jnp.arange(tile_count, dtype=jnp.int32)
    band = width // islands
    pieces = width // LANES
    moment_type = jnp.bfloat16 if band % 16 == 0 else jnp.float32
    levels = [spare, spare + 1, spare + 2, 2 * spare]
    levels = sorted(set(min(x, 2 * spare) for x in levels))

    def second_exchange(number, excess, of_pair, chosen):
        level = levels[number]
        most = (level + 1) // 2
        packed = place(excess, of_pair, chosen[:, :most].reshape(-1), "pack_spare")
        return exchange(
            [packed.reshape(islands, most * TILE, width)],
            ["half" if level % 2 else "peer_rows"],
            [(islands, spare * TILE, width)],
            islands,
            2 + number,
            "exchange_spare",
        )[0]

    firsts, seconds = [], []
    for step in range(STEPS):
        packed, excess, second, stats = filter_step(
            step,
            first,
            other,
            slot,
            send[step],
            excess_of[step],
            noise,
            series[step : step + 1],
            transition,
            obs_matrix,
            precision[None, :],
        )
        incoming, of_pair, bands, all_stats = exchange(
            [
                packed.reshape(islands, direct * TILE, width),
                excess,
                second.reshape(islands, band, width).astype(moment_type),
                stats,
            ],
            ["peer", "pair", "peer", "all"],
            [
                (islands, direct * TILE, width),
                excess.shape,
                (islands, band, width),
                (islands,) + stats.shape,
            ],
            islands,
            1,
            "exchange_tiles",
        )
        level = sum((need[step] > x).astype(jnp.int32) for x in levels[:-1])
        later = lax.switch(
            level,
            [functools.partial(second_exchange, number) for number in range(len(levels))],
            excess,
            of_pair,
            carried[step],
        )
        first = incoming.reshape(islands * direct, TILE, width)
        other = later.reshape(islands * spare, TILE, width)
        slot = source[step]
        total = jnp.sum(all_stats, axis=0)
        firsts.append(total[:pieces].reshape(width) / total[pieces, 0])
        seconds.append(jnp.sum(bands.astype(jnp.float32), axis=0) / total[pieces, 0])
    cloud = place(first, other, slot, "place_tiles").reshape(row_count, width)
    return (cloud, jnp.stack(firsts), jnp.stack(seconds))


def solution(mesh):
    return jax.shard_map(
        local,
        mesh=mesh,
        in_specs=(
            P(("groups", "isl"), None),
            P(None, ("groups", "isl"), None),
            P("groups", None),
            P(),
            P(),
            P(),
            P(None, ("groups", "isl"), None),
            P(None, ("groups", "isl")),
            P("groups"),
        ),
        out_specs=(P(("groups", "isl"), None), P("groups", None), P("groups", "isl", None)),
        check_vma=False,
    )
```

```python
import functools

import jax
import jax.numpy as jnp
from jax import lax
from jax.experimental import pallas as pl
from jax.experimental.pallas import tpu as pltpu
from jax.sharding import PartitionSpec as P

TILE = 128
STEPS = 3
LANES = 128
CHUNK = 16
MESH = pl.DeviceIdType.MESH


def greet_all(total, me, where):
    barrier = pltpu.get_barrier_semaphore()

    def greet(k, carry):
        pl.semaphore_signal(
            barrier, inc=1, device_id=where(lax.rem(me + k, total)), device_id_type=MESH
        )
        return carry

    lax.fori_loop(1, total, greet, 0)
    pl.semaphore_wait(barrier, total - 1)


def share_kernel(total, islands, table_ref, all_ref, send_sems, recv_sems, own_sem):
    me = lax.axis_index("groups") * islands + lax.axis_index("isl")

    def where(peer):
        return (peer // islands, lax.rem(peer, islands))

    greet_all(total, me, where)

    def remote(k):
        return pltpu.make_async_remote_copy(
            src_ref=table_ref,
            dst_ref=all_ref.at[me],
            send_sem=send_sems.at[k],
            recv_sem=recv_sems.at[k],
            device_id=where(lax.rem(me + k, total)),
            device_id_type=MESH,
        )

    def send(k, carry):
        remote(k).start()
        return carry

    def finish(k, carry):
        remote(k).wait()
        return carry

    lax.fori_loop(1, total, send, 0)
    own = pltpu.make_async_copy(table_ref, all_ref.at[me], own_sem)
    own.start()
    lax.fori_loop(1, total, finish, 0)
    own.wait()


def share_tables(table, groups, islands):
    total = groups * islands
    return pl.pallas_call(
        functools.partial(share_kernel, total, islands),
        out_shape=jax.ShapeDtypeStruct((total,) + table.shape, table.dtype),
        in_specs=[pl.BlockSpec(memory_space=pl.ANY)],
        out_specs=pl.BlockSpec(memory_space=pl.ANY),
        scratch_shapes=[
            pltpu.SemaphoreType.DMA((total,)),
            pltpu.SemaphoreType.DMA((total,)),
            pltpu.SemaphoreType.DMA,
        ],
        compiler_params=pltpu.CompilerParams(collective_id=0, has_side_effects=True),
        name="share_tables",
    )(table)


def exchange_kernel(islands, kinds, *refs):
    count = len(kinds)
    sources, targets = refs[:count], refs[count : 2 * count]
    send_sems, recv_sems, own_sems = refs[2 * count :]
    me = lax.axis_index("isl")
    sibling = me + 1 - 2 * lax.rem(me, 2)
    greet_all(islands, me, lambda peer: {"isl": peer})

    def ends(a, k, peer):
        kind = kinds[a]
        if kind == "peer":
            return sources[a].at[peer], targets[a].at[me]
        if kind == "all":
            return sources[a], targets[a].at[me]
        rows = sources[a].shape[1]
        if kind == "half" and k % 2 == 1:
            rows -= TILE
        return sources[a].at[peer, pl.ds(0, rows)], targets[a].at[me, pl.ds(0, rows)]

    def remote(a, k):
        if kinds[a] == "pair":
            peer, source, target = sibling, sources[a], targets[a]
        else:
            peer = lax.rem(me + k, islands)
            source, target = ends(a, k, peer)
        return pltpu.make_async_remote_copy(
            src_ref=source,
            dst_ref=target,
            send_sem=send_sems.at[a, k],
            recv_sem=recv_sems.at[a, k],
            device_id={"isl": peer},
            device_id_type=MESH,
        )

    def own(a):
        source, target = ends(a, 0, me)
        return pltpu.make_async_copy(source, target, own_sems.at[a])

    plans = [
        (a, k)
        for k in range(1, islands)
        for a in range(count)
        if (kinds[a] != "pair" or k == 1)
        and not (kinds[a] == "half" and k % 2 == 1 and sources[a].shape[1] == TILE)
    ]
    for a, k in plans:
        remote(a, k).start()
    kept = [a for a in range(count) if kinds[a] != "pair"]
    for a in kept:
        own(a).start()
    for a, k in plans:
        remote(a, k).wait()
    for a in kept:
        own(a).wait()


def exchange(arrays, kinds, shapes, islands, collective_id, name):
    count = len(arrays)
    return pl.pallas_call(
        functools.partial(exchange_kernel, islands, kinds),
        out_shape=[jax.ShapeDtypeStruct(dims, x.dtype) for x, dims in zip(arrays, shapes)],
        in_specs=[pl.BlockSpec(memory_space=pl.ANY)] * count,
        out_specs=[pl.BlockSpec(memory_space=pl.ANY)] * count,
        scratch_shapes=[
            pltpu.SemaphoreType.DMA((count, islands)),
            pltpu.SemaphoreType.DMA((count, islands)),
            pltpu.SemaphoreType.DMA((count,)),
        ],
        compiler_params=pltpu.CompilerParams(collective_id=collective_id, has_side_effects=True),
        name=name,
    )(*arrays)


def fetch(first_ref, second_ref, index, target, sem):
    split = first_ref.shape[0]

    @pl.when(index < split)
    def _():
        pltpu.make_async_copy(first_ref.at[index], target, sem).start()

    @pl.when(index >= split)
    def _():
        pltpu.make_async_copy(second_ref.at[index - split], target, sem).start()


def filter_kernel(source_ref, send_ref, spare_ref, first_ref, other_ref, *refs):
    noise_ref, series_ref, transition_ref, obs_ref, precision_ref = refs[:5]
    packed_ref, excess_ref, second_ref, stats_ref, fetched, moved, fetch_sems, sem = refs[5:]
    i = pl.program_id(0)

    def prefetch(chunk, slot):
        for t in range(CHUNK):
            index = source_ref[chunk * CHUNK + t]
            fetch(first_ref, other_ref, index, fetched.at[slot, t], fetch_sems.at[slot])

    now = lax.rem(i, 2)

    @pl.when(i == 0)
    def _():
        prefetch(0, 0)

    @pl.when(i + 1 < pl.num_programs(0))
    def _():
        prefetch(i + 1, 1 - now)

    pltpu.make_async_copy(fetched.at[now], fetched.at[now], fetch_sems.at[now]).wait()
    width = transition_ref.shape[0]

    @pl.when(i == 0)
    def _():
        second_ref[...] = jnp.zeros_like(second_ref)
        stats_ref[...] = jnp.zeros_like(stats_ref)

    cloud = fetched[now].reshape(CHUNK * TILE, width)
    propagated = (
        jnp.dot(cloud, transition_ref[...], preferred_element_type=jnp.float32)
        + noise_ref[0].astype(jnp.float32)
    ).astype(jnp.bfloat16)
    moved[pl.ds(i * CHUNK, CHUNK)] = propagated.reshape(CHUNK, TILE, width)
    innovation = series_ref[...] - jnp.dot(
        propagated, obs_ref[...], preferred_element_type=jnp.float32
    )
    misfit = jnp.mean(innovation * innovation * precision_ref[...], axis=1, keepdims=True)
    likelihood = jnp.exp(-0.5 * misfit)
    scaled = propagated.astype(jnp.float32) * likelihood
    sums = jnp.sum(scaled, axis=0, keepdims=True)
    pieces = width // LANES
    for c in range(pieces):
        stats_ref[c : c + 1, :] += sums[:, c * LANES : (c + 1) * LANES]
    stats_ref[pieces : pieces + 1, :] += jnp.broadcast_to(
        jnp.sum(likelihood, axis=0, keepdims=True), (1, LANES)
    )
    second_ref[...] += lax.dot_general(
        scaled.astype(jnp.bfloat16),
        propagated,
        (((0,), (0,)), ((), ())),
        preferred_element_type=jnp.float32,
    )

    @pl.when(i == pl.num_programs(0) - 1)
    def _():
        def pack(k, carry):
            pltpu.make_async_copy(moved.at[send_ref[k]], packed_ref.at[k], sem.at[0]).start()
            return carry

        def pack_excess(k, carry):
            pltpu.make_async_copy(moved.at[spare_ref[k]], excess_ref.at[k], sem.at[1]).start()
            return carry

        lax.fori_loop(0, packed_ref.shape[0], pack, 0, unroll=8)
        lax.fori_loop(0, excess_ref.shape[0], pack_excess, 0, unroll=8)
        pltpu.make_async_copy(packed_ref, packed_ref, sem.at[0]).wait()
        pltpu.make_async_copy(excess_ref, excess_ref, sem.at[1]).wait()


def filter_step(
    step, first, other, source, send, spare, noise, series, transition, obs_matrix, precision
):
    width = transition.shape[0]
    tile_count = source.shape[0]
    rows = CHUNK * TILE
    whole = lambda i, *_: (0, 0)
    matmuls = 3 * 2 * tile_count * TILE * width * width
    return pl.pallas_call(
        filter_kernel,
        grid_spec=pltpu.PrefetchScalarGridSpec(
            num_scalar_prefetch=3,
            grid=(tile_count // CHUNK,),
            in_specs=[
                pl.BlockSpec(memory_space=pl.ANY),
                pl.BlockSpec(memory_space=pl.ANY),
                pl.BlockSpec((1, rows, width), lambda i, *_: (step, i, 0)),
                pl.BlockSpec((1, width), whole),
                pl.BlockSpec((width, width), whole),
                pl.BlockSpec((width, width), whole),
                pl.BlockSpec((1, width), whole),
            ],
            out_specs=[
                pl.BlockSpec(memory_space=pl.ANY),
                pl.BlockSpec(memory_space=pl.ANY),
                pl.BlockSpec((width, width), whole),
                pl.BlockSpec((8, LANES), whole),
            ],
            scratch_shapes=[
                pltpu.VMEM((2, CHUNK, TILE, width), jnp.bfloat16),
                pltpu.VMEM((tile_count, TILE, width), jnp.bfloat16),
                pltpu.SemaphoreType.DMA((2,)),
                pltpu.SemaphoreType.DMA((2,)),
            ],
        ),
        out_shape=[
            jax.ShapeDtypeStruct((send.shape[0], TILE, width), jnp.bfloat16),
            jax.ShapeDtypeStruct((spare.shape[0], TILE, width), jnp.bfloat16),
            jax.ShapeDtypeStruct((width, width), jnp.float32),
            jax.ShapeDtypeStruct((8, LANES), jnp.float32),
        ],
        compiler_params=pltpu.CompilerParams(vmem_limit_bytes=40 * 1024 * 1024),
        cost_estimate=pl.CostEstimate(
            flops=matmuls, bytes_accessed=5 * tile_count * TILE * width * 2, transcendentals=0
        ),
        name="filter_step",
    )(source, send, spare, first, other, noise, series, transition, obs_matrix, precision)


def place_kernel(source_ref, first_ref, other_ref, out_ref, fetched, sems):
    i = pl.program_id(0)

    def prefetch(chunk, slot):
        for t in range(CHUNK):
            index = source_ref[chunk * CHUNK + t]
            fetch(first_ref, other_ref, index, fetched.at[slot, t], sems.at[slot])

    now = lax.rem(i, 2)

    @pl.when(i == 0)
    def _():
        prefetch(0, 0)

    @pl.when(i + 1 < pl.num_programs(0))
    def _():
        prefetch(i + 1, 1 - now)

    pltpu.make_async_copy(fetched.at[now], fetched.at[now], sems.at[now]).wait()
    out_ref[...] = fetched[now]


def place(first, other, source, name):
    tile = first.shape[1:]
    return pl.pallas_call(
        place_kernel,
        grid_spec=pltpu.PrefetchScalarGridSpec(
            num_scalar_prefetch=1,
            grid=(source.shape[0] // CHUNK,),
            in_specs=[pl.BlockSpec(memory_space=pl.ANY)] * 2,
            out_specs=pl.BlockSpec((CHUNK,) + tile, lambda i, *_: (i, 0, 0)),
            scratch_shapes=[
                pltpu.VMEM((2, CHUNK) + tile, first.dtype),
                pltpu.SemaphoreType.DMA((2,)),
            ],
        ),
        out_shape=jax.ShapeDtypeStruct(source.shape + tile, first.dtype),
        compiler_params=pltpu.CompilerParams(vmem_limit_bytes=16 * 1024 * 1024),
        name=name,
    )(source, first, other)


def swap_upper(parents, bits, islands, halfway):
    upper = parents[:, :, halfway:]
    swapped = upper
    for bit in range(max(islands.bit_length() - 1, 1)):
        span = 1 << bit
        flipped = upper.reshape(-1, islands // (2 * span), 2, span, halfway)[:, :, ::-1]
        swapped = jnp.where((bits == bit)[:, None, None], flipped.reshape(upper.shape), swapped)
    return jnp.concatenate([parents[:, :, :halfway], swapped], axis=2)


def plan(tables, bits, group, me, islands, tile_count, direct, capacity):
    groups = bits.shape[0]
    spare = capacity - direct
    wanted = swap_upper(
        tables.reshape(groups * STEPS, islands, tile_count),
        bits.reshape(groups * STEPS),
        islands,
        tile_count // 2,
    )
    island_of = wanted // tile_count
    ids = jnp.arange(islands, dtype=jnp.int32)
    counts = jnp.sum((island_of[:, :, None, :] == ids[:, None]).astype(jnp.int32), axis=3)
    over = jnp.maximum(counts - direct, 0)
    by_chip = jnp.sum(over.reshape(groups, STEPS, islands, islands // 2, 2), axis=4)
    need = jnp.max(by_chip, axis=(0, 2, 3))

    mine = lambda x: lax.dynamic_index_in_dim(
        x.reshape((groups, STEPS) + x.shape[1:]), group, 0, keepdims=False
    )
    island, tile, over = mine(island_of), mine(wanted % tile_count), mine(over)
    before = jnp.arange(tile_count)[:, None] < jnp.arange(tile_count)[None, :]
    matches = island == me
    position = jnp.dot(
        matches.astype(jnp.bfloat16).reshape(STEPS * islands, tile_count),
        before.astype(jnp.bfloat16),
        preferred_element_type=jnp.float32,
    ).reshape(matches.shape)
    ranks = jnp.arange(capacity, dtype=jnp.float32)
    chosen = matches[:, :, None, :] & (position[:, :, None, :] == ranks[None, None, :, None])
    send = jnp.sum(jnp.where(chosen, tile[:, :, None, :], 0), axis=3)

    core = me % 2
    of_even = lax.dynamic_index_in_dim(over, me - core, 2, keepdims=False)[:, :, None]
    order = 2 * jnp.arange(spare, dtype=jnp.int32)[None, :] + ((core + ids) % 2)[:, None]
    from_odd = (order[None] >= of_even).astype(jnp.int32)
    rank = jnp.clip(order[None] - from_odd * of_even, 0, spare - 1)
    carried = (from_odd != core).astype(jnp.int32) * (islands * spare) + ids[:, None] * spare + rank

    own = lax.dynamic_index_in_dim(island, me, 1, keepdims=False)
    same = (own[:, :, None] == own[:, None, :]) & before[None]
    own_rank = jnp.sum(same.astype(jnp.int32), axis=1)
    to_me = lax.dynamic_index_in_dim(over, me, 1, keepdims=False)
    even_over = jnp.pad(to_me[:, :-1], ((0, 0), (1, 0))) * (ids % 2)
    offset = jnp.sum(jnp.where(own[:, :, None] == ids, even_over[:, None, :], 0), axis=2)
    later = own_rank - direct + offset
    carrier = own - own % 2 + (later + me) % 2
    source = jnp.where(
        own_rank < direct,
        own * direct + own_rank,
        islands * direct + carrier * spare + later // 2,
    )
    return (
        need,
        send[:, :, :direct].reshape(STEPS, -1),
        send[:, :, direct:].reshape(STEPS, -1),
        carried,
        source,
    )


def local(
    particles, noise, series, transition, obs_matrix, precision, src_island, src_tile, swap_bits
):
    groups, islands = lax.axis_size("groups"), lax.axis_size("isl")
    group, me = lax.axis_index("groups"), lax.axis_index("isl")
    row_count, width = particles.shape
    tile_count = row_count // TILE
    capacity = 2 * max(2, tile_count // islands)
    direct = capacity // 2
    spare = capacity - direct
    table = src_island[:, :, 0] * tile_count + src_tile
    table = jnp.concatenate([table, swap_bits[:, None]], axis=1)
    table = jnp.pad(table, ((0, 8 - STEPS), (0, LANES - 1 - tile_count)))
    tables = share_tables(table, groups, islands).reshape(groups, islands, 8, LANES)
    bits = tables[:, 0, :STEPS, tile_count]
    parents = jnp.swapaxes(tables[:, :, :STEPS, :tile_count], 1, 2)
    need, send, excess_of, carried, source = plan(
        parents, bits, group, me, islands, tile_count, direct, capacity
    )
    first = other = particles.reshape(tile_count, TILE, width)
    slot = jnp.arange(tile_count, dtype=jnp.int32)
    band = width // islands
    pieces = width // LANES
    moment_type = jnp.bfloat16 if band % 16 == 0 else jnp.float32
    levels = [spare, spare + 1, spare + 2, 2 * spare]
    levels = sorted(set(min(x, 2 * spare) for x in levels))

    def second_exchange(number, excess, of_pair, chosen):
        level = levels[number]
        most = (level + 1) // 2
        packed = place(excess, of_pair, chosen[:, :most].reshape(-1), "pack_spare")
        return exchange(
            [packed.reshape(islands, most * TILE, width)],
            ["half" if level % 2 else "peer_rows"],
            [(islands, spare * TILE, width)],
            islands,
            2 + number,
            "exchange_spare",
        )[0]

    firsts, seconds = [], []
    for step in range(STEPS):
        packed, excess, second, stats = filter_step(
            step,
            first,
            other,
            slot,
            send[step],
            excess_of[step],
            noise,
            series[step : step + 1],
            transition,
            obs_matrix,
            precision[None, :],
        )
        incoming, of_pair, bands, all_stats = exchange(
            [
                packed.reshape(islands, direct * TILE, width),
                excess,
                second.reshape(islands, band, width).astype(moment_type),
                stats,
            ],
            ["peer", "pair", "peer", "all"],
            [
                (islands, direct * TILE, width),
                excess.shape,
                (islands, band, width),
                (islands,) + stats.shape,
            ],
            islands,
            1,
            "exchange_tiles",
        )
        level = sum((need[step] > x).astype(jnp.int32) for x in levels[:-1])
        later = lax.switch(
            level,
            [functools.partial(second_exchange, number) for number in range(len(levels))],
            excess,
            of_pair,
            carried[step],
        )
        first = incoming.reshape(islands * direct, TILE, width)
        other = later.reshape(islands * spare, TILE, width)
        slot = source[step]
        total = jnp.sum(all_stats, axis=0)
        firsts.append(total[:pieces].reshape(width) / total[pieces, 0])
        seconds.append(jnp.sum(bands.astype(jnp.float32), axis=0) / total[pieces, 0])
    cloud = place(first, other, slot, "place_tiles").reshape(row_count, width)
    return (cloud, jnp.stack(firsts), jnp.stack(seconds))


def solution(mesh):
    return jax.shard_map(
        local,
        mesh=mesh,
        in_specs=(
            P(("groups", "isl"), None),
            P(None, ("groups", "isl"), None),
            P("groups", None),
            P(),
            P(),
            P(),
            P(None, ("groups", "isl"), None),
            P(None, ("groups", "isl")),
            P("groups"),
        ),
        out_specs=(P(("groups", "isl"), None), P("groups", None), P("groups", "isl", None)),
        check_vma=False,
    )
```
